32 devices in a mesh: groups: 1, row: 32 (over z, y, x, core).
Axes of the slice: x: 2, y: 2, z: 4, core: 2. Of those that a mesh axis runs over, the one named last changes fastest.
Arguments:
- pair: bfloat16 [640, 640, 128], P(('groups', 'row')), may hold values from -6 to 6
- edge_left: bfloat16 [640, 640, 128], P(('groups', 'row')), may hold values from -6 to 6
- edge_right: bfloat16 [640, 640, 128], P(('groups', 'row')), may hold values from -6 to 6
- out_grad: bfloat16 [640, 640, 128], P(('groups', 'row')), may hold values from -6 to 6
- token_count: int32 [1], P('groups'), may hold values from 320 to 640
- w_in: bfloat16 [128, 640], replicated, may hold values from -0.5 to 0.5
- w_out: bfloat16 [128, 128], replicated, may hold values from -0.5 to 0.5
Outputs:
- pair_grad: bfloat16 [640, 640, 128], P(('groups', 'row'))
- left_grad: bfloat16 [640, 640, 128], P(('groups', 'row'))
- right_grad: bfloat16 [640, 640, 128], P(('groups', 'row'))
The draws below stay inside these ranges and needn't reach their ends.
Inputs may be any that keep to these rules, and one draw needn't show every extreme that they name: `token_count`: tokens at positions at or beyond it are padding.
All inputs are finite; a program needn't handle non-finite values.
Results may differ from the reference program's by a relative error of at most 0.0071.
Values may be sent and summed in bfloat16 or wider, within the bound.
A program may use at most 256 MiB of HBM per device.

```python
import jax
import jax.numpy as jnp
from jax import lax

C = 128
N = 640


def block_levels(own_key, shape, split, smallest, high):
    factor_of = 1.0
    for position, shards_of in split:
        draws = jax.random.uniform(jax.random.fold_in(jax.random.fold_in(own_key, 6), position), (shards_of,), jnp.float32, smallest / len(split), high / len(split))
        factor_of = factor_of * jnp.repeat(jnp.exp(draws), shape[position] // shards_of).reshape((-1,) + (1,) * (len(shape) - 1 - position))
    return factor_of


def scatter_about(stream_key, shape, scale, reach, pieces=(), kind=jnp.bfloat16):
    gain = block_levels(stream_key, shape, pieces, -0.22, 0.18) if pieces else 1.0
    result = jax.random.normal(stream_key, shape, jnp.float32) * scale * gain
    return jnp.minimum(jnp.maximum(result, -reach), reach).astype(kind)


def setup_inputs(seed: int = 0, part: int = 0) -> dict:
    arg_keys = jax.random.split(jax.random.key(seed), 8)
    part_keys = jax.random.split(jax.random.fold_in(arg_keys[7], part), 8)
    return {
        "pair": scatter_about(part_keys[0], (N, N, C), 1.0, 6.0, ((0, 32),)),
        "edge_left": scatter_about(part_keys[1], (N, N, C), 1.0, 6.0, ((0, 32),)),
        "edge_right": scatter_about(part_keys[2], (N, N, C), 1.0, 6.0, ((0, 32),)),
        "out_grad": scatter_about(part_keys[3], (N, N, C), 1.0, 6.0, ((0, 32),)),
        "token_count": jax.random.randint(part_keys[4], (1,), N // 2, N + 1).astype(jnp.int32),
        "w_in": scatter_about(arg_keys[5], (C, 5 * C), C ** -0.5, 0.5),
        "w_out": scatter_about(arg_keys[6], (C, C), C ** -0.5, 0.5),
    }


def normalize(values):
    centred = values - lax.optimization_barrier(jnp.mean(values, axis=-1, keepdims=True))
    inverse = lax.rsqrt(lax.optimization_barrier(jnp.mean(centred * centred, axis=-1, keepdims=True)) + 1e-05)
    return (centred * inverse, inverse)

def norm_back(normed, inverse, upstream):
    first = lax.optimization_barrier(jnp.mean(upstream, axis=-1, keepdims=True))
    second = lax.optimization_barrier(jnp.mean(upstream * normed, axis=-1, keepdims=True))
    return inverse * (upstream - first - normed * second)

def reference(pair, edge_left, edge_right, out_grad, token_count, w_in, w_out):
    length = token_count[0]
    positions = jnp.arange(N, dtype=jnp.int32)
    present = (positions < length).astype(jnp.float32)
    pair_mask = (present[:, None] * present[None, :])[:, :, None]
    masked_a = edge_left.astype(jnp.float32) * pair_mask
    masked_b = edge_right.astype(jnp.float32) * pair_mask
    outer = jnp.einsum('ikc,jkc->ijc', masked_a, masked_b, precision=lax.Precision.HIGHEST).astype(jnp.bfloat16)
    outer_flat = outer.astype(jnp.float32).reshape(N * N, C)
    outer_normed, outer_inv = normalize(outer_flat)
    update = jnp.dot(outer_normed.astype(jnp.bfloat16), w_out, preferred_element_type=jnp.float32)
    pair_normed, pair_inv = normalize(pair.astype(jnp.float32).reshape(N * N, C))
    projected = jnp.dot(pair_normed.astype(jnp.bfloat16), w_in, preferred_element_type=jnp.float32)
    gate_a = jax.nn.sigmoid(projected[:, 0:C])
    value_a = projected[:, C:2 * C]
    gate_b = jax.nn.sigmoid(projected[:, 2 * C:3 * C])
    value_b = projected[:, 3 * C:4 * C]
    out_gate = jax.nn.sigmoid(projected[:, 4 * C:5 * C])
    upstream = out_grad.astype(jnp.float32).reshape(N * N, C)
    grad_update = (upstream * out_gate).astype(jnp.bfloat16)
    grad_gate = upstream * update * out_gate * (1.0 - out_gate)
    grad_normed = jnp.dot(grad_update, w_out.T, preferred_element_type=jnp.float32)
    grad_outer = norm_back(outer_normed, outer_inv, grad_normed).astype(jnp.bfloat16)
    grad_outer = grad_outer.astype(jnp.float32).reshape(N, N, C)
    left_grad = (pair_mask * jnp.einsum('ijc,jkc->ikc', grad_outer, masked_b, precision=lax.Precision.HIGHEST)).astype(jnp.bfloat16)
    right_grad = (pair_mask * jnp.einsum('ijc,ikc->jkc', grad_outer, masked_a, precision=lax.Precision.HIGHEST)).astype(jnp.bfloat16)
    flow_a = left_grad.astype(jnp.float32).reshape(N * N, C)
    flow_b = right_grad.astype(jnp.float32).reshape(N * N, C)
    grad_pre = jnp.concatenate([flow_a * value_a * gate_a * (1.0 - gate_a), flow_a * gate_a, flow_b * value_b * gate_b * (1.0 - gate_b), flow_b * gate_b, grad_gate], axis=1).astype(jnp.bfloat16)
    grad_pair_normed = jnp.dot(grad_pre, w_in.T, preferred_element_type=jnp.float32)
    pair_grad = norm_back(pair_normed, pair_inv, grad_pair_normed).astype(jnp.bfloat16).reshape(N, N, C)
    return (pair_grad, left_grad, right_grad)
```

```python
import jax
import jax.numpy as jnp
import numpy as np
from jax import lax
from jax.experimental import pallas as pl
from jax.experimental.pallas import tpu as pltpu
from jax.sharding import PartitionSpec as P

F32 = jnp.float32
BF16 = jnp.bfloat16
VMEM_BYTES = 56 * 1024 * 1024
BAND = 4
LANES = 128


def nn(left, right):
    return lax.dot_general(left, right, (((1,), (0,)), ((), ())), preferred_element_type=F32)


def nt(left, right):
    return lax.dot_general(left, right, (((1,), (1,)), ((), ())), preferred_element_type=F32)


def tn(left, right):
    return lax.dot_general(left, right, (((0,), (0,)), ((), ())), preferred_element_type=F32)


def normalize(values):
    centred = values - jnp.mean(values, axis=0, keepdims=True)
    inverse = lax.rsqrt(jnp.mean(centred * centred, axis=0, keepdims=True) + 1e-05)
    return (centred * inverse, inverse)


def norm_back(normed, inverse, upstream):
    first = jnp.mean(upstream, axis=0, keepdims=True)
    second = jnp.mean(upstream * normed, axis=0, keepdims=True)
    return inverse * (upstream - first - normed * second)


def owner_order(groups, per_group):
    size = groups * BAND * per_group
    source = np.arange(size).reshape(BAND, groups, per_group).transpose(1, 0, 2).reshape(-1)
    return np.eye(size, dtype=np.float32)[source]


def channel_order(per_group):
    size = LANES * per_group
    source = np.arange(size).reshape(LANES, per_group).transpose(1, 0).reshape(-1)
    return np.eye(size, dtype=np.float32)[source]


def valid_block(info_ref, shape, row):
    column = lax.broadcasted_iota(jnp.int32, shape, 1)
    return (column < info_ref[0]) & (row < info_ref[0])


def send_kernel(info_ref, order_ref, edge_ref, out_ref):
    groups, height, extent = out_ref.shape
    per_group = height // BAND
    wide = jnp.concatenate([edge_ref[i] for i in range(BAND)], axis=1)
    moved = nt(order_ref[...], wide)
    shape = moved.shape
    place = lax.broadcasted_iota(jnp.int32, shape, 0)
    row = info_ref[1] + pl.program_id(0) * BAND + lax.rem(lax.div(place, per_group), BAND)
    kept = jnp.where(valid_block(info_ref, shape, row), moved, 0.0)
    out_ref[...] = kept.astype(BF16).reshape(out_ref.shape)


def split_channels(order, source_ref, target_ref, per_group):
    extent = target_ref.shape[2]
    size = LANES * per_group

    for block in range(extent // LANES):
        rows = source_ref[pl.ds(block * size, size), :]
        target_ref[:, pl.ds(block * LANES, LANES), :] = (
            nn(order, rows).astype(BF16).reshape(per_group, LANES, extent)
        )


def join_channels(order_back, source_ref, target_ref):
    per_group, extent, _ = source_ref.shape
    size = LANES * per_group

    for block in range(extent // LANES):
        rows = source_ref[:, pl.ds(block * LANES, LANES), :].reshape(size, extent)
        target_ref[pl.ds(block * size, size), :] = nn(order_back, rows).astype(BF16)
    rest = target_ref.shape[0] - per_group * extent
    if rest:
        target_ref[pl.ds(per_group * extent, rest), :] = jnp.zeros((rest, extent), BF16)


def product_kernel(order_ref, back_ref, a_ref, b_ref, out_ref, chan_a_ref, chan_b_ref, work):
    per_group = chan_a_ref.shape[0]
    split_channels(order_ref[...], a_ref, chan_a_ref, per_group)
    split_channels(order_ref[...], b_ref, chan_b_ref, per_group)

    @pl.loop(0, per_group)
    def _(chan):
        work[chan] = nt(chan_a_ref[chan], chan_b_ref[chan]).astype(BF16)

    join_channels(back_ref[...], work, out_ref)


def left_kernel(order_ref, back_ref, grad_ref, chan_b_ref, out_ref, chan_grad_ref, work):
    per_group = chan_b_ref.shape[0]
    split_channels(order_ref[...], grad_ref, chan_grad_ref, per_group)

    @pl.loop(0, per_group)
    def _(chan):
        work[chan] = nn(chan_grad_ref[chan], chan_b_ref[chan]).astype(BF16)

    join_channels(back_ref[...], work, out_ref)


def right_kernel(back_ref, chan_grad_ref, chan_a_ref, out_ref, work):
    per_group = chan_a_ref.shape[0]

    @pl.loop(0, per_group)
    def _(chan):
        work[chan] = tn(chan_grad_ref[chan], chan_a_ref[chan]).astype(BF16)

    join_channels(back_ref[...], work, out_ref)


def middle_kernel(
    info_ref, order_ref, back_ref, eye_ref, gate_ref, w_out_ref, w_out_t_ref,
    outer_ref, pair_ref, upstream_ref, grad_ref, gate_grad_ref,
):
    groups, height, extent = outer_ref.shape
    chans = pair_ref.shape[2]
    outers = nn(back_ref[...], outer_ref[...].reshape(groups * height, extent))
    eye = eye_ref[...]
    pieces = []
    for i in range(BAND):
        outer_normed, outer_inv = normalize(outers[i * chans : (i + 1) * chans])
        pair_normed, _ = normalize(nt(eye, pair_ref[i]))
        upstream = nt(eye, upstream_ref[i])
        out_gate = jax.nn.sigmoid(nn(gate_ref[...], pair_normed.astype(BF16)))
        update = nn(w_out_t_ref[...], outer_normed.astype(BF16))
        opened = upstream * out_gate
        gate_grad_ref[i] = (opened * update * (1.0 - out_gate)).astype(BF16)
        grad_normed = nn(w_out_ref[...], opened.astype(BF16))
        grad = norm_back(outer_normed, outer_inv, grad_normed)
        row = info_ref[1] + pl.program_id(0) * BAND + i
        pieces.append(jnp.where(valid_block(info_ref, grad.shape, row), grad, 0.0).astype(BF16))
    grads = nn(order_ref[...], jnp.concatenate(pieces, axis=0))
    grad_ref[...] = grads.astype(BF16).reshape(grad_ref.shape)


def final_kernel(
    back_ref, eye_ref, w_in_ref, w_in_t_ref, left_ref, right_ref, pair_ref, gate_grad_ref,
    pair_grad_ref, left_grad_ref, right_grad_ref,
):
    groups, height, extent = left_ref.shape
    chans = pair_ref.shape[2]
    width = pair_grad_ref.shape[1]
    lefts = nn(back_ref[...], left_ref[...].reshape(groups * height, extent))
    rights = nn(back_ref[...], right_ref[...].reshape(groups * height, extent))
    eye = eye_ref[...]
    for i in range(BAND):
        flow_a = lefts[i * chans : (i + 1) * chans]
        flow_b = rights[i * chans : (i + 1) * chans]
        pair_normed, pair_inv = normalize(nt(eye, pair_ref[i]))
        projected = nn(w_in_t_ref[...], pair_normed.astype(BF16))
        gate_a = jax.nn.sigmoid(projected[0:chans])
        value_a = projected[chans : 2 * chans]
        gate_b = jax.nn.sigmoid(projected[2 * chans : 3 * chans])
        value_b = projected[3 * chans : 4 * chans]
        through_a = flow_a * gate_a
        through_b = flow_b * gate_b
        grad_pre = jnp.concatenate(
            [
                (through_a * value_a * (1.0 - gate_a)).astype(BF16),
                through_a.astype(BF16),
                (through_b * value_b * (1.0 - gate_b)).astype(BF16),
                through_b.astype(BF16),
                gate_grad_ref[i],
            ],
            axis=0,
        )
        grad = norm_back(pair_normed, pair_inv, nn(w_in_ref[...], grad_pre))
        for ref, value in ((pair_grad_ref, grad), (left_grad_ref, flow_a), (right_grad_ref, flow_b)):
            ref[i, pl.ds(0, extent), :] = value.T.astype(BF16)
            if width > extent:
                ref[i, pl.ds(extent, width - extent), :] = jnp.zeros((width - extent, chans), BF16)


def local_at(extent, pair, edge_left, edge_right, out_grad, info, w_in, w_out):
    rows, width, chans = pair.shape
    groups = lax.axis_size("row")
    per_group = chans // groups
    height = BAND * per_group
    steps = rows // BAND
    params = pltpu.CompilerParams(vmem_limit_bytes=VMEM_BYTES)
    to_owner = owner_order(groups, per_group)
    order = jnp.asarray(to_owner, BF16)
    back = jnp.asarray(to_owner.T, BF16)
    by_chan = channel_order(per_group)
    chan_order = jnp.asarray(by_chan, BF16)
    chan_back = jnp.asarray(by_chan.T, BF16)
    eye = jnp.eye(chans, dtype=BF16)

    smem = pl.BlockSpec(memory_space=pltpu.SMEM)
    vmem = pl.BlockSpec(memory_space=pltpu.VMEM)
    row_block = pl.BlockSpec((BAND, extent, chans), lambda i: (i, 0, 0))
    full_block = pl.BlockSpec((BAND, width, chans), lambda i: (i, 0, 0))
    gate_block = pl.BlockSpec((BAND, chans, extent), lambda i: (i, 0, 0))
    group_block = pl.BlockSpec((groups, height, extent), lambda i: (0, i, 0))
    group_shape = jax.ShapeDtypeStruct((groups, rows * per_group, extent), BF16)
    flat_shape = jax.ShapeDtypeStruct((groups * rows * per_group, extent), BF16)
    chan_shape = jax.ShapeDtypeStruct((per_group, extent, extent), BF16)
    full_shape = jax.ShapeDtypeStruct((rows, width, chans), BF16)
    work = pltpu.VMEM((per_group, extent, extent), BF16)
    size = rows * extent * chans * 2

    def cost(units, flops):
        return pl.CostEstimate(flops=flops, bytes_accessed=units * size, transcendentals=0)

    def exchange(tensor):
        return lax.all_to_all(tensor.reshape(group_shape.shape), "row", split_axis=0, concat_axis=0, tiled=True)

    def send(edge):
        return pl.pallas_call(
            send_kernel, grid=(steps,), out_shape=group_shape,
            in_specs=[smem, vmem, row_block], out_specs=group_block,
            compiler_params=params, cost_estimate=cost(2, 2 * 512 * rows * extent * chans),
            name="send_edge",
        )(info, order, edge)

    chan_a = exchange(send(edge_left))
    chan_b = exchange(send(edge_right))
    cube = 2 * per_group * extent**3
    product, chan_a, chan_b = pl.pallas_call(
        product_kernel, out_shape=(flat_shape, chan_shape, chan_shape),
        in_specs=[vmem] * 4, out_specs=(vmem,) * 3, scratch_shapes=[work],
        compiler_params=params, cost_estimate=cost(5, 3 * cube), name="product",
    )(chan_order, chan_back, chan_a.reshape(flat_shape.shape), chan_b.reshape(flat_shape.shape))
    outer = exchange(product)
    grad, gate_grad = pl.pallas_call(
        middle_kernel, grid=(steps,),
        out_shape=(group_shape, jax.ShapeDtypeStruct((rows, chans, extent), BF16)),
        in_specs=[smem] + [vmem] * 6 + [group_block, row_block, row_block],
        out_specs=(group_block, gate_block),
        compiler_params=params, cost_estimate=cost(5, 4 * cube), name="middle",
    )(info, order, back, eye, w_in[:, 4 * chans :].T, w_out, w_out.T, outer, pair, out_grad)
    grad = exchange(grad)
    left, chan_grad = pl.pallas_call(
        left_kernel, out_shape=(flat_shape, chan_shape),
        in_specs=[vmem] * 4, out_specs=(vmem,) * 2, scratch_shapes=[work],
        compiler_params=params, cost_estimate=cost(4, 3 * cube), name="left",
    )(chan_order, chan_back, grad.reshape(flat_shape.shape), chan_b)
    left = exchange(left)
    right = pl.pallas_call(
        right_kernel, out_shape=flat_shape,
        in_specs=[vmem] * 3, out_specs=vmem, scratch_shapes=[work],
        compiler_params=params, cost_estimate=cost(3, 2 * cube), name="right",
    )(chan_back, chan_grad, chan_a)
    right = exchange(right)
    return pl.pallas_call(
        final_kernel, grid=(steps,), out_shape=(full_shape,) * 3,
        in_specs=[vmem] * 4 + [group_block, group_block, row_block, gate_block],
        out_specs=(full_block,) * 3,
        compiler_params=params, cost_estimate=cost(7, 5 * cube), name="final",
    )(back, eye, w_in, w_in[:, : 4 * chans].T, left, right, pair, gate_grad)


def local(pair, edge_left, edge_right, out_grad, token_count, w_in, w_out):
    rows, width, _ = pair.shape
    length = token_count[0]
    info = jnp.stack([length, lax.axis_index("row") * rows]).astype(jnp.int32)
    longest = length if lax.axis_size("groups") == 1 else lax.pmax(length, "groups")
    extents = [e for e in range(3 * LANES, width, LANES)] + [width]
    index = sum((longest > e).astype(jnp.int32) for e in extents[:-1])

    def branch(extent):
        return lambda *operands: local_at(extent, *operands)

    return lax.switch(
        index, [branch(e) for e in extents],
        pair, edge_left, edge_right, out_grad, info, w_in, w_out,
    )


def solution(mesh):
    split = P(("groups", "row"), None, None)
    return jax.shard_map(
        local, mesh=mesh,
        in_specs=(split, split, split, split, P("groups"), P(), P()),
        out_specs=(split, split, split), check_vma=False,
    )
```

```python
import functools

import jax
import jax.numpy as jnp
import numpy as np
from jax import lax
from jax.experimental import pallas as pl
from jax.experimental.pallas import tpu as pltpu
from jax.sharding import PartitionSpec as P

F32 = jnp.float32
BF16 = jnp.bfloat16
VMEM_BYTES = 56 * 1024 * 1024
BAND = 4
LANES = 128
PLACES = 64


def nn(left, right):
    return lax.dot_general(left, right, (((1,), (0,)), ((), ())), preferred_element_type=F32)


def nt(left, right):
    return lax.dot_general(left, right, (((1,), (1,)), ((), ())), preferred_element_type=F32)


def tn(left, right):
    return lax.dot_general(left, right, (((0,), (0,)), ((), ())), preferred_element_type=F32)


def normalize(values):
    centred = values - jnp.mean(values, axis=0, keepdims=True)
    inverse = lax.rsqrt(jnp.mean(centred * centred, axis=0, keepdims=True) + 1e-05)
    return (centred * inverse, inverse)


def norm_back(normed, inverse, upstream):
    first = jnp.mean(upstream, axis=0, keepdims=True)
    second = jnp.mean(upstream * normed, axis=0, keepdims=True)
    return inverse * (upstream - first - normed * second)


def owner_order(groups, per_group):
    size = groups * BAND * per_group
    source = np.arange(size).reshape(BAND, groups, per_group).transpose(1, 0, 2).reshape(-1)
    return np.eye(size, dtype=np.float32)[source]


def channel_order(per_group):
    size = PLACES * per_group
    source = np.arange(size).reshape(PLACES, per_group).transpose(1, 0).reshape(-1)
    return np.eye(size, dtype=np.float32)[source]


def valid_block(info_ref, shape, row):
    column = lax.broadcasted_iota(jnp.int32, shape, 1)
    return (column < info_ref[0]) & (row < info_ref[0])


def send_kernel(info_ref, order_ref, edge_ref, out_ref):
    groups, height, extent = out_ref.shape
    per_group = height // BAND
    wide = jnp.concatenate([edge_ref[i] for i in range(BAND)], axis=1)
    moved = nt(order_ref[...], wide)
    shape = moved.shape
    place = lax.broadcasted_iota(jnp.int32, shape, 0)
    row = info_ref[1] + pl.program_id(0) * BAND + lax.rem(lax.div(place, per_group), BAND)
    kept = jnp.where(valid_block(info_ref, shape, row), moved, 0.0)
    out_ref[...] = kept.astype(BF16).reshape(out_ref.shape)


def exchange_kernel(near_ref, wide_ref, near_out, wide_out, near_send, near_recv, wide_send, wide_recv, own):
    me = lax.axis_index("row")
    half = near_ref.shape[0]
    count = 2 * half
    place = lax.rem(me, half)
    base = me - place
    blocks = wide_ref.shape[0]

    def there(target):
        return {"device_id": {"row": target}, "device_id_type": pl.DeviceIdType.MESH}

    barrier = pltpu.get_barrier_semaphore()

    @pl.loop(1, count)
    def _(step):
        pl.semaphore_signal(barrier, inc=1, **there(lax.rem(me + step, count)))

    pl.semaphore_wait(barrier, count - 1)

    def near_copy(step):
        slot = lax.rem(place + lax.rem(step * 11, half), half)
        return pltpu.make_async_remote_copy(
            src_ref=near_ref.at[slot], dst_ref=near_out.at[place],
            send_sem=near_send.at[step], recv_sem=near_recv.at[step], **there(base + slot),
        )

    def wide_copy(step):
        target = lax.rem(me + lax.rem(step * 11, count), count)
        return pltpu.make_async_remote_copy(
            src_ref=wide_ref.at[lax.rem(target, blocks)], dst_ref=wide_out.at[me],
            send_sem=wide_send.at[step], recv_sem=wide_recv.at[step], **there(target),
        )

    near_own = pltpu.make_async_copy(near_ref.at[place], near_out.at[place], own.at[0])
    wide_own = pltpu.make_async_copy(wide_ref.at[lax.rem(me, blocks)], wide_out.at[me], own.at[1])

    @pl.loop(1, half)
    def _(step):
        wide_copy(step).start()
        near_copy(step).start()

    @pl.loop(half, count)
    def _(step):
        wide_copy(step).start()

    near_own.start()
    wide_own.start()

    @pl.loop(1, half)
    def _(step):
        near_copy(step).wait()

    @pl.loop(1, count)
    def _(step):
        wide_copy(step).wait()

    near_own.wait()
    wide_own.wait()


def exchange_both(near, wide, collective_id):
    half = near.shape[0]
    count = 2 * half
    sems = [pltpu.SemaphoreType.DMA((n,)) for n in (half, half, count, count, 2)]
    hbm = pl.BlockSpec(memory_space=pl.ANY)
    return pl.pallas_call(
        exchange_kernel,
        out_shape=(
            jax.ShapeDtypeStruct(near.shape, near.dtype),
            jax.ShapeDtypeStruct((count,) + wide.shape[1:], wide.dtype),
        ),
        in_specs=[hbm, hbm], out_specs=(hbm, hbm), scratch_shapes=sems,
        compiler_params=pltpu.CompilerParams(collective_id=collective_id, has_side_effects=True),
        name="exchange",
    )(near, wide)


def split_channels(order, source_ref, target_ref):
    per_group, places, extent = target_ref.shape
    size = PLACES * per_group

    @pl.loop(0, places // PLACES)
    def _(block):
        rows = source_ref[pl.ds(pl.multiple_of(block * size, size), size), :]
        target_ref[:, pl.ds(pl.multiple_of(block * PLACES, PLACES), PLACES), :] = (
            nn(order, rows).astype(BF16).reshape(per_group, PLACES, extent)
        )


def join_channels(order_back, source_ref, target_ref):
    per_group, places, extent = source_ref.shape
    size = PLACES * per_group

    @pl.loop(0, places // PLACES)
    def _(block):
        rows = source_ref[:, pl.ds(pl.multiple_of(block * PLACES, PLACES), PLACES), :]
        target_ref[pl.ds(pl.multiple_of(block * size, size), size), :] = (
            nn(order_back, rows.reshape(size, extent)).astype(BF16)
        )

    rest = target_ref.shape[0] - per_group * places
    if rest:
        target_ref[pl.ds(per_group * places, rest), :] = jnp.zeros((rest, extent), BF16)


def product_kernel(order_ref, back_ref, a_ref, b_ref, out_ref, chan_a_ref, chan_b_ref, work):
    split_channels(order_ref[...], a_ref, chan_a_ref)
    split_channels(order_ref[...], b_ref, chan_b_ref)

    @pl.loop(0, chan_a_ref.shape[0])
    def _(chan):
        work[chan] = nt(chan_a_ref[chan], chan_b_ref[chan]).astype(BF16)

    join_channels(back_ref[...], work, out_ref)


def left_kernel(order_ref, back_ref, grad_ref, chan_b_ref, out_ref, chan_grad_ref, work):
    split_channels(order_ref[...], grad_ref, chan_grad_ref)

    @pl.loop(0, chan_b_ref.shape[0])
    def _(chan):
        work[chan] = nn(chan_grad_ref[chan], chan_b_ref[chan]).astype(BF16)

    join_channels(back_ref[...], work, out_ref)


def right_kernel(back_ref, chan_grad_ref, chan_a_ref, out_ref, work):
    @pl.loop(0, chan_a_ref.shape[0])
    def _(chan):
        work[chan] = tn(chan_grad_ref[chan], chan_a_ref[chan]).astype(BF16)

    join_channels(back_ref[...], work, out_ref)


def middle_kernel(
    info_ref, order_ref, back_ref, eye_ref, gate_ref, w_out_ref, w_out_t_ref,
    outer_ref, pair_ref, upstream_ref, grad_ref, gate_grad_ref,
):
    groups, height, extent = outer_ref.shape
    chans = pair_ref.shape[2]
    outers = nn(back_ref[...], outer_ref[...].reshape(groups * height, extent))
    eye = eye_ref[...]
    pieces = []
    for i in range(BAND):
        outer_normed, outer_inv = normalize(outers[i * chans : (i + 1) * chans])
        pair_normed, _ = normalize(nt(eye, pair_ref[i]))
        upstream = nt(eye, upstream_ref[i])
        out_gate = jax.nn.sigmoid(nn(gate_ref[...], pair_normed.astype(BF16)))
        update = nn(w_out_t_ref[...], outer_normed.astype(BF16))
        opened = upstream * out_gate
        gate_grad_ref[i] = (opened * update * (1.0 - out_gate)).astype(BF16)
        grad_normed = nn(w_out_ref[...], opened.astype(BF16))
        grad = norm_back(outer_normed, outer_inv, grad_normed)
        row = info_ref[1] + pl.program_id(0) * BAND + i
        pieces.append(jnp.where(valid_block(info_ref, grad.shape, row), grad, 0.0).astype(BF16))
    grads = nn(order_ref[...], jnp.concatenate(pieces, axis=0))
    grad_ref[...] = grads.astype(BF16).reshape(grad_ref.shape)


def final_kernel(
    back_ref, eye_ref, w_in_ref, w_in_t_ref, left_ref, right_ref, pair_ref, gate_grad_ref,
    pair_grad_ref, left_grad_ref, right_grad_ref,
):
    groups, height, extent = left_ref.shape
    chans = pair_ref.shape[2]
    width = pair_grad_ref.shape[1]
    lefts = nn(back_ref[...], left_ref[...].reshape(groups * height, extent))
    rights = nn(back_ref[...], right_ref[pl.ds(0, groups)].reshape(groups * height, extent))
    rights += nn(back_ref[...], right_ref[pl.ds(groups, groups)].reshape(groups * height, extent))
    rights = rights.astype(BF16).astype(F32)
    eye = eye_ref[...]
    for i in range(BAND):
        flow_a = lefts[i * chans : (i + 1) * chans]
        flow_b = rights[i * chans : (i + 1) * chans]
        pair_normed, pair_inv = normalize(nt(eye, pair_ref[i]))
        projected = nn(w_in_t_ref[...], pair_normed.astype(BF16))
        gate_a = jax.nn.sigmoid(projected[0:chans])
        value_a = projected[chans : 2 * chans]
        gate_b = jax.nn.sigmoid(projected[2 * chans : 3 * chans])
        value_b = projected[3 * chans : 4 * chans]
        through_a = flow_a * gate_a
        through_b = flow_b * gate_b
        grad_pre = jnp.concatenate(
            [
                (through_a * value_a * (1.0 - gate_a)).astype(BF16),
                through_a.astype(BF16),
                (through_b * value_b * (1.0 - gate_b)).astype(BF16),
                through_b.astype(BF16),
                gate_grad_ref[i],
            ],
            axis=0,
        )
        grad = norm_back(pair_normed, pair_inv, nn(w_in_ref[...], grad_pre))
        for ref, value in ((pair_grad_ref, grad), (left_grad_ref, flow_a), (right_grad_ref, flow_b)):
            ref[i, pl.ds(0, extent), :] = value.T.astype(BF16)
            if width > extent:
                ref[i, pl.ds(extent, width - extent), :] = jnp.zeros((width - extent, chans), BF16)


def local_at(extent, first_id, pair, edge_left, edge_right, out_grad, info, w_in, w_out):
    rows, width, chans = pair.shape
    count = lax.axis_size("row")
    groups = count // 2
    halves = [list(range(groups)), list(range(groups, count))]
    per_group = chans // groups
    band_rows = rows * groups
    height = BAND * per_group
    steps = rows // BAND
    params = pltpu.CompilerParams(vmem_limit_bytes=VMEM_BYTES)
    to_owner = owner_order(groups, per_group)
    order = jnp.asarray(to_owner, BF16)
    back = jnp.asarray(to_owner.T, BF16)
    by_chan = channel_order(per_group)
    chan_order = jnp.asarray(by_chan, BF16)
    chan_back = jnp.asarray(by_chan.T, BF16)
    eye = jnp.eye(chans, dtype=BF16)

    smem = pl.BlockSpec(memory_space=pltpu.SMEM)
    vmem = pl.BlockSpec(memory_space=pltpu.VMEM)
    row_block = pl.BlockSpec((BAND, extent, chans), lambda i: (i, 0, 0))
    full_block = pl.BlockSpec((BAND, width, chans), lambda i: (i, 0, 0))
    gate_block = pl.BlockSpec((BAND, chans, extent), lambda i: (i, 0, 0))
    group_block = pl.BlockSpec((groups, height, extent), lambda i: (0, i, 0))
    group_shape = jax.ShapeDtypeStruct((groups, rows * per_group, extent), BF16)
    flat_shape = jax.ShapeDtypeStruct((groups * rows * per_group, extent), BF16)
    wide_block = pl.BlockSpec((count, height, extent), lambda i: (0, i, 0))
    wide_shape = jax.ShapeDtypeStruct((count * rows * per_group, extent), BF16)
    chan_shape = jax.ShapeDtypeStruct((per_group, extent, extent), BF16)
    half_shape = jax.ShapeDtypeStruct((per_group, band_rows, extent), BF16)
    full_shape = jax.ShapeDtypeStruct((rows, width, chans), BF16)
    work = pltpu.VMEM(chan_shape.shape, BF16)
    half_work = pltpu.VMEM(half_shape.shape, BF16)
    size = rows * extent * chans * 2

    def cost(units, flops):
        return pl.CostEstimate(flops=flops, bytes_accessed=units * size, transcendentals=0)

    def exchange(tensor):
        return lax.all_to_all(
            tensor.reshape(group_shape.shape), "row", split_axis=0, concat_axis=0, tiled=True,
            axis_index_groups=halves,
        )

    def send(edge):
        return pl.pallas_call(
            send_kernel, grid=(steps,), out_shape=group_shape,
            in_specs=[smem, vmem, row_block], out_specs=group_block,
            compiler_params=params, cost_estimate=cost(2, 2 * 512 * rows * extent * chans),
            name="send_edge",
        )(info, order, edge)

    chan_a, chan_b = exchange_both(send(edge_left), send(edge_right), first_id)
    cube = 2 * per_group * band_rows * extent**2
    product, chan_a, chan_b = pl.pallas_call(
        product_kernel, out_shape=(flat_shape, half_shape, chan_shape),
        in_specs=[vmem] * 4, out_specs=(vmem,) * 3, scratch_shapes=[half_work],
        compiler_params=params, cost_estimate=cost(5, 3 * cube), name="product",
    )(chan_order, chan_back, chan_a.reshape(flat_shape.shape), chan_b.reshape(wide_shape.shape))
    outer = exchange(product)
    grad, gate_grad = pl.pallas_call(
        middle_kernel, grid=(steps,),
        out_shape=(group_shape, jax.ShapeDtypeStruct((rows, chans, extent), BF16)),
        in_specs=[smem] + [vmem] * 6 + [group_block, row_block, row_block],
        out_specs=(group_block, gate_block),
        compiler_params=params, cost_estimate=cost(5, 4 * cube), name="middle",
    )(info, order, back, eye, w_in[:, 4 * chans :].T, w_out, w_out.T, outer, pair, out_grad)
    grad = exchange(grad)
    left, chan_grad = pl.pallas_call(
        left_kernel, out_shape=(flat_shape, half_shape),
        in_specs=[vmem] * 4, out_specs=(vmem,) * 2, scratch_shapes=[half_work],
        compiler_params=params, cost_estimate=cost(4, 3 * cube), name="left",
    )(chan_order, chan_back, grad.reshape(flat_shape.shape), chan_b)
    right = pl.pallas_call(
        right_kernel, out_shape=wide_shape,
        in_specs=[vmem] * 3, out_specs=vmem, scratch_shapes=[work],
        compiler_params=params, cost_estimate=cost(3, 2 * cube), name="right",
    )(chan_back, chan_grad, chan_a)
    left, right = exchange_both(
        left.reshape(group_shape.shape),
        right.reshape((count,) + group_shape.shape[1:]), first_id + 1,
    )
    return pl.pallas_call(
        final_kernel, grid=(steps,), out_shape=(full_shape,) * 3,
        in_specs=[vmem] * 4 + [group_block, wide_block, row_block, gate_block],
        out_specs=(full_block,) * 3,
        compiler_params=params, cost_estimate=cost(7, 5 * cube), name="final",
    )(back, eye, w_in, w_in[:, : 4 * chans].T, left, right, pair, gate_grad)


def local(pair, edge_left, edge_right, out_grad, token_count, w_in, w_out):
    rows, width, _ = pair.shape
    length = token_count[0]
    info = jnp.stack([length, lax.axis_index("row") * rows]).astype(jnp.int32)
    longest = length if lax.axis_size("groups") == 1 else lax.pmax(length, "groups")
    extents = [e for e in range(3 * LANES, width, LANES)] + [width]
    index = sum((longest > e).astype(jnp.int32) for e in extents[:-1])

    def branch(place):
        return functools.partial(local_at, extents[place], 2 * place)

    return lax.switch(
        index, [branch(i) for i in range(len(extents))],
        pair, edge_left, edge_right, out_grad, info, w_in, w_out,
    )


def solution(mesh):
    split = P(("groups", "row"), None, None)
    return jax.shard_map(
        local, mesh=mesh,
        in_specs=(split, split, split, split, P("groups"), P(), P()),
        out_specs=(split, split, split), check_vma=False,
    )
```

```python
import functools

import jax
import jax.numpy as jnp
import numpy as np
from jax import lax
from jax.experimental import pallas as pl
from jax.experimental.pallas import tpu as pltpu
from jax.sharding import PartitionSpec as P

F32 = jnp.float32
BF16 = jnp.bfloat16
VMEM_BYTES = 56 * 1024 * 1024
BAND = 4
LANES = 128
PLACES = 64


def nn(left, right):
    return lax.dot_general(left, right, (((1,), (0,)), ((), ())), preferred_element_type=F32)


def nt(left, right):
    return lax.dot_general(left, right, (((1,), (1,)), ((), ())), preferred_element_type=F32)


def tn(left, right):
    return lax.dot_general(left, right, (((0,), (0,)), ((), ())), preferred_element_type=F32)


def normalize(values):
    centred = values - jnp.mean(values, axis=0, keepdims=True)
    inverse = lax.rsqrt(jnp.mean(centred * centred, axis=0, keepdims=True) + 1e-05)
    return (centred * inverse, inverse)


def norm_back(normed, inverse, upstream):
    first = jnp.mean(upstream, axis=0, keepdims=True)
    second = jnp.mean(upstream * normed, axis=0, keepdims=True)
    return inverse * (upstream - first - normed * second)


def owner_order(groups, per_group):
    size = groups * BAND * per_group
    source = np.arange(size).reshape(BAND, groups, per_group).transpose(1, 0, 2).reshape(-1)
    return np.eye(size, dtype=np.float32)[source]


def channel_order(per_group):
    size = PLACES * per_group
    source = np.arange(size).reshape(PLACES, per_group).transpose(1, 0).reshape(-1)
    return np.eye(size, dtype=np.float32)[source]


def valid_block(info_ref, shape, row):
    column = lax.broadcasted_iota(jnp.int32, shape, 1)
    return (column < info_ref[0]) & (row < info_ref[0])


def send_kernel(info_ref, order_ref, edge_ref, out_ref):
    groups, height, extent = out_ref.shape
    per_group = height // BAND
    wide = jnp.concatenate([edge_ref[i] for i in range(BAND)], axis=1)
    moved = nt(order_ref[...], wide)
    shape = moved.shape
    place = lax.broadcasted_iota(jnp.int32, shape, 0)
    row = info_ref[1] + pl.program_id(0) * BAND + lax.rem(lax.div(place, per_group), BAND)
    kept = jnp.where(valid_block(info_ref, shape, row), moved, 0.0)
    out_ref[...] = kept.astype(BF16).reshape(out_ref.shape)


def exchange_kernel(near_ref, wide_ref, near_out, wide_out, *sems):
    exchange(near_ref.at, wide_ref, near_out, wide_out, None, *sems)


def left_exchange_kernel(back_ref, chan_grad_ref, chan_b_ref, wide_ref, near_out, wide_out, work, near, *sems):
    height = near_out.shape[1]

    def fill():
        @pl.loop(0, chan_b_ref.shape[0])
        def _(chan):
            work[chan] = nn(chan_grad_ref[chan], chan_b_ref[chan]).astype(BF16)

        join_channels(back_ref[...], work, near)

    exchange(Bands(near, height), wide_ref, near_out, wide_out, fill, *sems)


class Bands:
    def __init__(self, ref, height):
        self.ref, self.height = ref, height

    def __getitem__(self, block):
        start = pl.multiple_of(block * self.height, self.height)
        return self.ref.at[pl.ds(start, self.height), :]


def exchange(near_blocks, wide_ref, near_out, wide_out, fill, near_send, near_recv, wide_send, wide_recv, own):
    me = lax.axis_index("row")
    half = near_out.shape[0]
    count = 2 * half
    place = lax.rem(me, half)
    base = me - place
    blocks = wide_ref.shape[0]

    def there(target):
        return {"device_id": {"row": target}, "device_id_type": pl.DeviceIdType.MESH}

    barrier = pltpu.get_barrier_semaphore()

    @pl.loop(1, count)
    def _(step):
        pl.semaphore_signal(barrier, inc=1, **there(lax.rem(me + step, count)))

    pl.semaphore_wait(barrier, count - 1)

    def near_copy(step):
        slot = lax.rem(place + lax.rem(step * 11, half), half)
        return pltpu.make_async_remote_copy(
            src_ref=near_blocks[slot], dst_ref=near_out.at[place],
            send_sem=near_send.at[step], recv_sem=near_recv.at[step], **there(base + slot),
        )

    def wide_copy(step):
        target = lax.rem(me + lax.rem(step * 11, count), count)
        return pltpu.make_async_remote_copy(
            src_ref=wide_ref.at[lax.rem(target, blocks)], dst_ref=wide_out.at[me],
            send_sem=wide_send.at[step], recv_sem=wide_recv.at[step], **there(target),
        )

    near_own = pltpu.make_async_copy(near_blocks[place], near_out.at[place], own.at[0])
    wide_own = pltpu.make_async_copy(wide_ref.at[lax.rem(me, blocks)], wide_out.at[me], own.at[1])

    if fill is None:
        @pl.loop(1, half)
        def _(step):
            wide_copy(step).start()
            near_copy(step).start()

        @pl.loop(half, count)
        def _(step):
            wide_copy(step).start()

        wide_own.start()
    else:
        @pl.loop(1, count)
        def _(step):
            wide_copy(step).start()

        wide_own.start()
        fill()

        @pl.loop(1, half)
        def _(step):
            near_copy(step).start()

    near_own.start()

    @pl.loop(1, half)
    def _(step):
        near_copy(step).wait()

    @pl.loop(1, count)
    def _(step):
        wide_copy(step).wait()

    near_own.wait()
    wide_own.wait()


def exchange_both(near, wide, collective_id):
    half = near.shape[0]
    count = 2 * half
    sems = [pltpu.SemaphoreType.DMA((n,)) for n in (half, half, count, count, 2)]
    hbm = pl.BlockSpec(memory_space=pl.ANY)
    return pl.pallas_call(
        exchange_kernel,
        out_shape=(
            jax.ShapeDtypeStruct(near.shape, near.dtype),
            jax.ShapeDtypeStruct((count,) + wide.shape[1:], wide.dtype),
        ),
        in_specs=[hbm, hbm], out_specs=(hbm, hbm), scratch_shapes=sems,
        compiler_params=pltpu.CompilerParams(collective_id=collective_id, has_side_effects=True),
        name="exchange",
    )(near, wide)


def split_channels(order, source_ref, target_ref):
    per_group, places, extent = target_ref.shape
    size = PLACES * per_group

    @pl.loop(0, places // PLACES)
    def _(block):
        rows = source_ref[pl.ds(pl.multiple_of(block * size, size), size), :]
        target_ref[:, pl.ds(pl.multiple_of(block * PLACES, PLACES), PLACES), :] = (
            nn(order, rows).astype(BF16).reshape(per_group, PLACES, extent)
        )


def join_channels(order_back, source_ref, target_ref):
    per_group, places, extent = source_ref.shape
    size = PLACES * per_group

    @pl.loop(0, places // PLACES)
    def _(block):
        rows = source_ref[:, pl.ds(pl.multiple_of(block * PLACES, PLACES), PLACES), :]
        target_ref[pl.ds(pl.multiple_of(block * size, size), size), :] = (
            nn(order_back, rows.reshape(size, extent)).astype(BF16)
        )

    rest = target_ref.shape[0] - per_group * places
    if rest:
        target_ref[pl.ds(per_group * places, rest), :] = jnp.zeros((rest, extent), BF16)


def product_kernel(order_ref, back_ref, a_ref, b_ref, out_ref, chan_a_ref, chan_b_ref, work):
    split_channels(order_ref[...], a_ref, chan_a_ref)
    split_channels(order_ref[...], b_ref, chan_b_ref)

    @pl.loop(0, chan_a_ref.shape[0])
    def _(chan):
        work[chan] = nt(chan_a_ref[chan], chan_b_ref[chan]).astype(BF16)

    join_channels(back_ref[...], work, out_ref)


def right_kernel(order_ref, back_ref, grad_ref, chan_a_ref, out_ref, chan_grad_ref, work):
    split_channels(order_ref[...], grad_ref, chan_grad_ref)

    @pl.loop(0, chan_a_ref.shape[0])
    def _(chan):
        work[chan] = tn(chan_grad_ref[chan], chan_a_ref[chan]).astype(BF16)

    join_channels(back_ref[...], work, out_ref)


def middle_kernel(
    info_ref, order_ref, back_ref, eye_ref, gate_ref, w_out_ref, w_out_t_ref,
    outer_ref, pair_ref, upstream_ref, grad_ref, gate_grad_ref,
):
    groups, height, extent = outer_ref.shape
    chans = pair_ref.shape[2]
    outers = nn(back_ref[...], outer_ref[...].reshape(groups * height, extent))
    eye = eye_ref[...]
    pieces = []
    for i in range(BAND):
        outer_normed, outer_inv = normalize(outers[i * chans : (i + 1) * chans])
        pair_normed, _ = normalize(nt(eye, pair_ref[i]))
        upstream = nt(eye, upstream_ref[i])
        out_gate = jax.nn.sigmoid(nn(gate_ref[...], pair_normed.astype(BF16)))
        update = nn(w_out_t_ref[...], outer_normed.astype(BF16))
        opened = upstream * out_gate
        gate_grad_ref[i] = (opened * update * (1.0 - out_gate)).astype(BF16)
        grad_normed = nn(w_out_ref[...], opened.astype(BF16))
        grad = norm_back(outer_normed, outer_inv, grad_normed)
        row = info_ref[1] + pl.program_id(0) * BAND + i
        pieces.append(jnp.where(valid_block(info_ref, grad.shape, row), grad, 0.0).astype(BF16))
    grads = nn(order_ref[...], jnp.concatenate(pieces, axis=0))
    grad_ref[...] = grads.astype(BF16).reshape(grad_ref.shape)


def final_kernel(
    back_ref, eye_ref, w_in_ref, w_in_t_ref, left_ref, right_ref, pair_ref, gate_grad_ref,
    pair_grad_ref, left_grad_ref, right_grad_ref,
):
    groups, height, extent = left_ref.shape
    chans = pair_ref.shape[2]
    width = pair_grad_ref.shape[1]
    lefts = nn(back_ref[...], left_ref[...].reshape(groups * height, extent))
    rights = nn(back_ref[...], right_ref[pl.ds(0, groups)].reshape(groups * height, extent))
    rights += nn(back_ref[...], right_ref[pl.ds(groups, groups)].reshape(groups * height, extent))
    rights = rights.astype(BF16).astype(F32)
    eye = eye_ref[...]
    for i in range(BAND):
        flow_a = lefts[i * chans : (i + 1) * chans]
        flow_b = rights[i * chans : (i + 1) * chans]
        pair_normed, pair_inv = normalize(nt(eye, pair_ref[i]))
        projected = nn(w_in_t_ref[...], pair_normed.astype(BF16))
        gate_a = jax.nn.sigmoid(projected[0:chans])
        value_a = projected[chans : 2 * chans]
        gate_b = jax.nn.sigmoid(projected[2 * chans : 3 * chans])
        value_b = projected[3 * chans : 4 * chans]
        through_a = flow_a * gate_a
        through_b = flow_b * gate_b
        grad_pre = jnp.concatenate(
            [
                (through_a * value_a * (1.0 - gate_a)).astype(BF16),
                through_a.astype(BF16),
                (through_b * value_b * (1.0 - gate_b)).astype(BF16),
                through_b.astype(BF16),
                gate_grad_ref[i],
            ],
            axis=0,
        )
        grad = norm_back(pair_normed, pair_inv, nn(w_in_ref[...], grad_pre))
        for ref, value in ((pair_grad_ref, grad), (left_grad_ref, flow_a), (right_grad_ref, flow_b)):
            ref[i, pl.ds(0, extent), :] = value.T.astype(BF16)
            if width > extent:
                ref[i, pl.ds(extent, width - extent), :] = jnp.zeros((width - extent, chans), BF16)


def local_at(extent, first_id, pair, edge_left, edge_right, out_grad, info, w_in, w_out):
    rows, width, chans = pair.shape
    count = lax.axis_size("row")
    groups = count // 2
    halves = [list(range(groups)), list(range(groups, count))]
    per_group = chans // groups
    band_rows = rows * groups
    height = BAND * per_group
    steps = rows // BAND
    params = pltpu.CompilerParams(vmem_limit_bytes=VMEM_BYTES)
    to_owner = owner_order(groups, per_group)
    order = jnp.asarray(to_owner, BF16)
    back = jnp.asarray(to_owner.T, BF16)
    by_chan = channel_order(per_group)
    chan_order = jnp.asarray(by_chan, BF16)
    chan_back = jnp.asarray(by_chan.T, BF16)
    eye = jnp.eye(chans, dtype=BF16)

    smem = pl.BlockSpec(memory_space=pltpu.SMEM)
    vmem = pl.BlockSpec(memory_space=pltpu.VMEM)
    row_block = pl.BlockSpec((BAND, extent, chans), lambda i: (i, 0, 0))
    full_block = pl.BlockSpec((BAND, width, chans), lambda i: (i, 0, 0))
    gate_block = pl.BlockSpec((BAND, chans, extent), lambda i: (i, 0, 0))
    group_block = pl.BlockSpec((groups, height, extent), lambda i: (0, i, 0))
    group_shape = jax.ShapeDtypeStruct((groups, rows * per_group, extent), BF16)
    flat_shape = jax.ShapeDtypeStruct((groups * rows * per_group, extent), BF16)
    wide_block = pl.BlockSpec((count, height, extent), lambda i: (0, i, 0))
    wide_shape = jax.ShapeDtypeStruct((count * rows * per_group, extent), BF16)
    chan_shape = jax.ShapeDtypeStruct((per_group, extent, extent), BF16)
    half_shape = jax.ShapeDtypeStruct((per_group, band_rows, extent), BF16)
    full_shape = jax.ShapeDtypeStruct((rows, width, chans), BF16)
    work = pltpu.VMEM(chan_shape.shape, BF16)
    half_work = pltpu.VMEM(half_shape.shape, BF16)
    size = rows * extent * chans * 2

    def cost(units, flops):
        return pl.CostEstimate(flops=flops, bytes_accessed=units * size, transcendentals=0)

    def regroup(tensor):
        return lax.all_to_all(
            tensor.reshape(group_shape.shape), "row", split_axis=0, concat_axis=0, tiled=True,
            axis_index_groups=halves,
        )

    def send(edge):
        return pl.pallas_call(
            send_kernel, grid=(steps,), out_shape=group_shape,
            in_specs=[smem, vmem, row_block], out_specs=group_block,
            compiler_params=params, cost_estimate=cost(2, 2 * 512 * rows * extent * chans),
            name="send_edge",
        )(info, order, edge)

    chan_a, chan_b = exchange_both(send(edge_left), send(edge_right), first_id)
    cube = 2 * per_group * band_rows * extent**2
    product, chan_a, chan_b = pl.pallas_call(
        product_kernel, out_shape=(flat_shape, half_shape, chan_shape),
        in_specs=[vmem] * 4, out_specs=(vmem,) * 3, scratch_shapes=[half_work],
        compiler_params=params, cost_estimate=cost(5, 3 * cube), name="product",
    )(chan_order, chan_back, chan_a.reshape(flat_shape.shape), chan_b.reshape(wide_shape.shape))
    outer = regroup(product)
    grad, gate_grad = pl.pallas_call(
        middle_kernel, grid=(steps,),
        out_shape=(group_shape, jax.ShapeDtypeStruct((rows, chans, extent), BF16)),
        in_specs=[smem] + [vmem] * 6 + [group_block, row_block, row_block],
        out_specs=(group_block, gate_block),
        compiler_params=params, cost_estimate=cost(5, 4 * cube), name="middle",
    )(info, order, back, eye, w_in[:, 4 * chans :].T, w_out, w_out.T, outer, pair, out_grad)
    grad = regroup(grad)
    right, chan_grad = pl.pallas_call(
        right_kernel, out_shape=(wide_shape, half_shape),
        in_specs=[vmem] * 4, out_specs=(vmem,) * 2, scratch_shapes=[work],
        compiler_params=params, cost_estimate=cost(5, 3 * cube), name="right",
    )(chan_order, chan_back, grad.reshape(flat_shape.shape), chan_a)
    wide = (count,) + group_shape.shape[1:]
    hbm = pl.BlockSpec(memory_space=pl.ANY)
    left, right = pl.pallas_call(
        left_exchange_kernel,
        out_shape=(group_shape, jax.ShapeDtypeStruct(wide, BF16)),
        in_specs=[vmem] * 3 + [hbm], out_specs=(hbm, hbm),
        scratch_shapes=[half_work, pltpu.VMEM(flat_shape.shape, BF16)]
        + [pltpu.SemaphoreType.DMA((n,)) for n in (groups, groups, count, count, 2)],
        compiler_params=pltpu.CompilerParams(
            vmem_limit_bytes=VMEM_BYTES, collective_id=first_id + 1, has_side_effects=True
        ),
        name="left_exchange",
    )(chan_back, chan_grad, chan_b, right.reshape(wide))
    return pl.pallas_call(
        final_kernel, grid=(steps,), out_shape=(full_shape,) * 3,
        in_specs=[vmem] * 4 + [group_block, wide_block, row_block, gate_block],
        out_specs=(full_block,) * 3,
        compiler_params=params, cost_estimate=cost(7, 5 * cube), name="final",
    )(back, eye, w_in, w_in[:, : 4 * chans].T, left, right, pair, gate_grad)


def local(pair, edge_left, edge_right, out_grad, token_count, w_in, w_out):
    rows, width, _ = pair.shape
    length = token_count[0]
    info = jnp.stack([length, lax.axis_index("row") * rows]).astype(jnp.int32)
    longest = length if lax.axis_size("groups") == 1 else lax.pmax(length, "groups")
    extents = [e for e in range(3 * LANES, width, LANES)] + [width]
    index = sum((longest > e).astype(jnp.int32) for e in extents[:-1])

    def branch(place):
        return functools.partial(local_at, extents[place], 2 * place)

    return lax.switch(
        index, [branch(i) for i in range(len(extents))],
        pair, edge_left, edge_right, out_grad, info, w_in, w_out,
    )


def solution(mesh):
    split = P(("groups", "row"), None, None)
    return jax.shard_map(
        local, mesh=mesh,
        in_specs=(split, split, split, split, P("groups"), P(), P()),
        out_specs=(split, split, split), check_vma=False,
    )
```
